256 devices in a mesh: tis: 32 (over y_lo, z, core), ves: 8 (over y_hi, x).
Axes of the slice: x: 4, y: 4 (y_hi: 2, y_lo: 2; y = y_hi * 2 + y_lo), z: 8, core: 2. Of those that a mesh axis runs over, the one named last changes fastest.
Arguments:
- point_xyz: float32 [3, 131072], P(None, 'tis'), may hold values from 0 to 1
- point_cell: int32 [131072], P('tis'), may hold values from 0 to 127, never falling along the last dimension, each value on 1 to 4096 neighbouring positions
- seg_xyz: float32 [3, 32768], P(None, 'ves'), may hold values from 0 to 1
- seg_radius: float32 [32768], P('ves'), may hold values from 0.004 to 0.02
- conductance: float32 [32768], P('ves'), may hold values from 0.5 to 2
- flow_inv: float32 [32768], P('ves'), may hold values from 0.1 to 0.5
- parent: int32 [32768], P('ves'), may hold values from 0 to 32767, as said below
- inflow: float32 [8, 32768], P(None, 'ves'), may hold values from 2 to 4
- rate_table: float32 [8, 128], replicated, may hold values from 0.5 to 2
- half_sat: float32 [8], replicated, may hold values from 0.3 to 1
- diffusivity: float32 [8], replicated, may hold values from 0.5 to 2
- base_level: float32 [8], replicated, may hold values from -0.5 to 0.5
- sources: float32 [8, 32768], P(None, 'ves'), may hold values from 0.5 to 2
- contents: float32 [8, 32768], P(None, 'ves'), may hold values from 1 to 3
Outputs:
- tissue_level: float32 [8, 131072], P(None, 'tis')
- seg_sources: float32 [8, 32768], P(None, 'ves')
- blood_content: float32 [8, 32768], P(None, 'ves')
The draws below stay inside these ranges and needn't reach their ends.
Inputs may be any that keep to these rules, and one draw needn't show every extreme that they name: Each segment is a root (parent equals its own index) or its parent lies among the 4096 segments before it: j - 4096 <= parent[j] < j. Points are ordered by region: point_cell never falls along the points.
All inputs are finite; a program needn't handle non-finite values.
Results may differ from the reference program's by a relative error of at most 0.0003.
Values sent between devices are 32-bit elements; how exact they have to be, the bound alone decides.
A program may use at most 128 MiB of HBM per device.

```python
import math
import jax
import jax.numpy as jnp
import numpy as np
from jax import lax

SOL = 8
PT_DEV = 4096
SEG_DEV = 4096
ITERS = 3
CELLS = 128
NP = 131072
NS = 32768
N_TIS = 32


path_count = 4


def vessel_midpoints(key, reach, wiggle):
    base = jax.random.fold_in(key, 23)
    keys = jax.random.split(base, 6)
    start = jax.random.uniform(keys[0], (3, path_count), minval=0.0, maxval=1.0)
    heading = jax.random.uniform(keys[1], (3, path_count), minval=-1.0, maxval=1.0)
    heading = heading / jnp.sqrt(jnp.sum(heading * heading, axis=0, keepdims=True) + 0.05)
    amplitude = wiggle * jax.random.uniform(keys[2], (3, path_count, 3), minval=0.5, maxval=1.5)
    phase = jax.random.uniform(keys[3], (3, path_count, 3), minval=0.0, maxval=2.0 * math.pi)
    which = jax.random.randint(keys[4], (NS,), 0, path_count)
    along = jax.random.uniform(keys[5], (NS,), minval=0.0, maxval=1.0)
    harmonic = jnp.arange(1, 4, dtype=jnp.float32)
    raw = start[:, which] + reach * along[None, :] * heading[:, which]
    wave = amplitude[:, which, :] * jnp.sin(2.0 * math.pi * harmonic[None, None, :] * along[None, :, None] + phase[:, which, :])
    raw = raw + jnp.sum(wave, axis=2)
    return (1.0 - jnp.abs(jnp.mod(raw, 2.0) - 1.0)).astype(jnp.float32)


def draw_seg_xyz(key, part):
    reach, wiggle = (1.5, 0.02)
    return vessel_midpoints(key, reach, wiggle)


def draw_point_xyz(key, part):
    reach, wiggle = (1.5, 0.02)
    midpoints = vessel_midpoints(key, reach, wiggle)
    keys = jax.random.split(jax.random.fold_in(key, 29), 5)
    picked = jax.random.randint(keys[0], (NP,), 0, NS)
    offset = jnp.exp(jax.random.uniform(keys[1], (NP,), minval=math.log(0.06), maxval=math.log(0.3)))
    near_share = 0.95
    direction = jax.random.normal(keys[2], (3, NP))
    direction = direction / jnp.sqrt(jnp.sum(direction * direction, axis=0, keepdims=True) + 0.001)
    nearby = midpoints[:, picked] + offset[None, :] * direction
    faraway = jax.random.uniform(keys[3], (3, NP), minval=0.0, maxval=1.0)
    mixing = jax.random.uniform(keys[4], (NP,), minval=0.0, maxval=1.0) < near_share
    placed = jnp.where(mixing[None, :], nearby, faraway)
    return jnp.clip(placed, 0.0, 1.0).astype(jnp.float32)


def draw_parent(key, part):
    first_key, second_key = jax.random.split(jax.random.fold_in(key, 11))
    seg_index = jnp.arange(NS, dtype=jnp.int32)
    distance = jax.random.randint(first_key, (NS,), 1, SEG_DEV + 1)
    root_pick = jax.random.randint(second_key, (NS,), 0, 8)
    candidate = seg_index - distance
    return jnp.where((root_pick == 0) | (candidate < 0), seg_index, candidate).astype(jnp.int32)


def block_levels(stream_key, dims, pieces, smallest, high):
    loudness = 1.0
    for position, shards_of in pieces:
        steps = jax.random.uniform(jax.random.fold_in(jax.random.fold_in(stream_key, 6), position), (shards_of,), jnp.float32, smallest / len(pieces), high / len(pieces))
        loudness = loudness * jnp.repeat(jnp.exp(steps), dims[position] // shards_of).reshape((-1,) + (1,) * (len(dims) - 1 - position))
    return loudness


def split_up(amount, total, most, slope):
    loads = [(1 << 20) // math.isqrt(rank ** slope) + 1 for rank in range(2, amount + 1)]
    surplus, holding = total - most - (amount - 1), [1] * (amount - 1)
    while surplus > 0:
        candidates = [i for i in range(amount - 1) if holding[i] < most]
        whole, left = sum([loads[i] for i in candidates]), surplus
        for i in candidates:
            extra = min(most - holding[i], max(1, left * loads[i] // whole), surplus)
            holding[i] = holding[i] + extra
            surplus = surplus - extra
    return np.array([most] + holding)


def uneven(stream_key, count, total, limit, slope):
    if count == 2:
        one = jax.random.randint(stream_key, (), max(1, total - limit), min(limit, total - 1) + 1)
        return jnp.stack([one, total - one])
    lengths = jnp.asarray(split_up(count, total, limit, slope), jnp.int32)
    couples = (count - 1) // 2
    giver, receiver = lengths[1:1 + 2 * couples:2], lengths[2:2 + 2 * couples:2]
    slack = jnp.minimum(giver - 1, limit - receiver)
    moved = jax.random.randint(jax.random.fold_in(stream_key, 1), (couples,), 0, 1 << 20) % (slack + 1)
    lengths = lengths.at[1:1 + 2 * couples:2].set(giver - moved).at[2:2 + 2 * couples:2].set(receiver + moved)
    return lengths[jax.random.permutation(jax.random.fold_in(stream_key, 2), count)]


def setup_inputs(seed: int = 0) -> dict:
    arg_keys = jax.random.split(jax.random.key(seed), 15)
    return {
        "point_xyz": draw_point_xyz(jax.random.fold_in(arg_keys[14], 71), 0),
        "point_cell": jnp.searchsorted(jnp.cumsum(uneven(arg_keys[1], CELLS, NP, PT_DEV, 1)), jnp.arange(NP), side="right").astype(jnp.int32),
        "seg_xyz": draw_seg_xyz(jax.random.fold_in(arg_keys[14], 71), 0),
        "seg_radius": jnp.clip(jnp.exp(math.log(0.02) - 1.6094378 * jax.random.uniform(arg_keys[3], (NS,), jnp.float32) ** block_levels(arg_keys[3], (NS,), ((0, 8),), -0.2, 0.2)), 0.004, 0.02),
        "conductance": jnp.clip(jnp.exp(math.log(2.0) - 1.3862944 * jax.random.uniform(arg_keys[4], (NS,), jnp.float32) ** block_levels(arg_keys[4], (NS,), ((0, 8),), -0.2, 0.2)), 0.5, 2.0),
        "flow_inv": jnp.clip(jnp.exp(math.log(0.5) - 1.609438 * jax.random.uniform(arg_keys[5], (NS,), jnp.float32) ** block_levels(arg_keys[5], (NS,), ((0, 8),), -0.2, 0.2)), 0.1, 0.5),
        "parent": draw_parent(jax.random.fold_in(arg_keys[14], 71), 0),
        "inflow": jnp.clip(2.0 + 2.0 * jax.random.uniform(arg_keys[7], (SOL, NS), jnp.float32) ** block_levels(arg_keys[7], (SOL, NS), ((1, 8),), -0.2, 0.2), 2.0, 4.0),
        "rate_table": jnp.clip(jnp.exp(jax.random.uniform(arg_keys[8], (SOL, CELLS), jnp.float32, math.log(0.5), math.log(2.0))), 0.5, 2.0),
        "half_sat": jnp.clip(jnp.exp(jax.random.uniform(arg_keys[9], (SOL,), jnp.float32, math.log(0.3), math.log(1.0))), 0.3, 1.0),
        "diffusivity": jnp.clip(jnp.exp(jax.random.uniform(arg_keys[10], (SOL,), jnp.float32, math.log(0.5), math.log(2.0))), 0.5, 2.0),
        "base_level": jnp.clip(jax.random.uniform(arg_keys[11], (SOL,), jnp.float32, -0.5, 0.5), -0.5, 0.5),
        "sources": jnp.clip(0.5 + 1.5 * jax.random.uniform(arg_keys[12], (SOL, NS), jnp.float32) ** block_levels(arg_keys[12], (SOL, NS), ((1, 8),), -0.2, 0.2), 0.5, 2.0),
        "contents": jnp.clip(1.0 + 2.0 * jax.random.uniform(arg_keys[13], (SOL, NS), jnp.float32) ** block_levels(arg_keys[13], (SOL, NS), ((1, 8),), -0.2, 0.2), 1.0, 3.0),
    }


RELAX = 0.5
BALANCE = 0.5

def kernel_rows(points, seg_pos, radius):
    dist_sq = (points[0][:, None] - seg_pos[0][None, :]) ** 2
    dist_sq = dist_sq + (points[1][:, None] - seg_pos[1][None, :]) ** 2
    dist_sq = dist_sq + (points[2][:, None] - seg_pos[2][None, :]) ** 2
    return lax.rsqrt(dist_sq + (radius * radius)[None, :]).astype(jnp.bfloat16)

def reference(point_xyz, point_cell, seg_xyz, seg_radius, conductance, flow_inv, parent, inflow, rate_table, half_sat, diffusivity, base_level, sources, contents):
    rates = jnp.take(rate_table, point_cell, axis=1)
    point_blocks = point_xyz.reshape(3, N_TIS, PT_DEV).transpose(1, 0, 2)
    rate_blocks = rates.reshape(SOL, N_TIS, PT_DEV).transpose(1, 0, 2)
    seg_index = jnp.arange(NS, dtype=jnp.int32)
    tissue_level = jnp.zeros((SOL, NP), jnp.float32)
    for sweep in range(ITERS):
        src_bf = sources.astype(jnp.bfloat16)

        def one_block(totals, inputs):
            pts_block, rate_block = inputs
            kernel_tile = kernel_rows(pts_block, seg_xyz, seg_radius)
            raw_sum = lax.dot_general(src_bf, kernel_tile, (((1,), (1,)), ((), ())), preferred_element_type=jnp.float32)
            level = base_level[:, None] + raw_sum / (diffusivity[:, None] * NS)
            sink_field = rate_block * level / (jnp.abs(level) + half_sat[:, None])
            wall_acc = totals[0] + jnp.dot(sink_field.astype(jnp.bfloat16), kernel_tile, preferred_element_type=jnp.float32)
            return ((wall_acc, totals[1] + lax.optimization_barrier(jnp.sum(sink_field, axis=1))), level)
        init = (jnp.zeros((SOL, NS), jnp.float32), jnp.zeros((SOL,), jnp.float32))
        (wall_raw, sink_total), levels = lax.scan(one_block, init, (point_blocks, rate_blocks))
        tissue_level = levels.transpose(1, 0, 2).reshape(SOL, NP)
        source_total = lax.optimization_barrier(jnp.sum(sources, axis=1))
        outflow = contents - sources * flow_inv[None, :]
        contents = jnp.where((parent == seg_index)[None, :], inflow, jnp.take(outflow, parent, axis=1))
        wall_field = wall_raw / (diffusivity[:, None] * NP)
        sources = RELAX * sources + RELAX * conductance[None, :] * (contents - wall_field)
        base_level = base_level + BALANCE * (source_total / NS - sink_total / NP)
    return (tissue_level, sources, contents)
```

```python
import functools

import jax
import jax.numpy as jnp
from jax import lax
from jax.experimental import pallas as pl
from jax.experimental.pallas import tpu as pltpu
from jax.sharding import PartitionSpec as P

ITERS = 3
RELAX = 0.5
BALANCE = 0.5
LANES = 128
FEATURES = 128
MESH = pl.DeviceIdType.MESH


def pieces(x):
    high = x.astype(jnp.bfloat16).astype(jnp.float32)
    rest = x - high
    middle = rest.astype(jnp.bfloat16).astype(jnp.float32)
    return high, middle, (rest - middle).astype(jnp.bfloat16).astype(jnp.float32)


def dot(a, b):
    return jnp.dot(a, b, preferred_element_type=jnp.float32)


def dot_nt(a, b):
    return lax.dot_general(a, b, (((1,), (1,)), ((), ())), preferred_element_type=jnp.float32)


def at(i, size):
    return pl.ds(pl.multiple_of(i * size, size), size)


def kernel(
    n_ves,
    n_z,
    pts,
    segs,
    point_ref,
    cell_ref,
    seg_ref,
    radius_ref,
    cond_ref,
    flow_ref,
    parent_ref,
    inflow_ref,
    table_ref,
    half_ref,
    diff_ref,
    base_ref,
    sources_ref,
    contents_ref,
    level_out,
    sources_out,
    contents_out,
    tile,
    point_feat,
    seg_feat,
    feat,
    rates,
    base,
    t_sum,
    t_send,
    t_recv,
    level,
    sink,
    sink_sum,
    wall,
    a_send,
    a_recv,
    b_send,
    b_recv,
    src,
    cont,
    joined,
    t_ss,
    t_rs,
    l_ss,
    l_rs,
    a_ss,
    a_rs,
    b_ss,
    b_rs,
    z_ss,
    z_rs,
    c_ss,
    c_rs,
    o_ss,
    o_rs,
):
    f32, bf16 = jnp.float32, jnp.bfloat16
    n_tis = 4 * n_z
    chunk = pts // n_ves
    quarter = segs // 4
    n_chunks = segs // LANES
    per_q = n_z
    total_pts = pts * n_tis
    total_segs = segs * n_ves
    t, v = lax.axis_index("tis"), lax.axis_index("ves")
    y, z, core = t // (2 * n_z), (t // 2) % n_z, t % 2

    def quarter_of(m):
        return ((y + m // 2) % 2) * 2 + (core + m % 2) % 2

    def tis_near(m):
        return ((y + m // 2) % 2) * (2 * n_z) + z * 2 + (core + m % 2) % 2

    def tis_along(k):
        return y * (2 * n_z) + ((z + k) % n_z) * 2 + core

    def ves_at(k):
        return (v + k) % n_ves

    def send_ves(k, a, b, s, r):
        return pltpu.make_async_remote_copy(
            src_ref=a, dst_ref=b, send_sem=s, recv_sem=r, device_id={"ves": ves_at(k)}, device_id_type=MESH
        )

    def send_tis(to, a, b, s, r):
        return pltpu.make_async_remote_copy(
            src_ref=a, dst_ref=b, send_sem=s, recv_sem=r, device_id={"tis": to}, device_id_type=MESH
        )

    def t_copy(it, k):
        return send_ves(k, t_send.at[k], t_recv.at[it, k - 1], t_ss.at[k - 1], t_rs.at[it, k - 1])

    def l_copy(it, k, of):
        return send_ves(k, level.at[it, of], level.at[it, of], l_ss.at[k - 1], l_rs.at[it, k - 1])

    def a_copy(it, m):
        return send_tis(tis_near(m), a_send.at[m], a_recv.at[it, m - 1], a_ss.at[m - 1], a_rs.at[it, m - 1])

    def b_copy(it, k):
        return send_tis(
            tis_along(k), b_send.at[(z + k) % n_z], b_recv.at[it, k - 1], b_ss.at[k - 1], b_rs.at[it, k - 1]
        )

    def z_copy(it, k, of):
        place = src.at[it + 1, quarter_of(0), of]
        return send_tis(tis_along(k), place, place, z_ss.at[k - 1], z_rs.at[it, k - 1])

    def c_copy(it, m, of):
        place = src.at[it + 1, of]
        return send_tis(tis_near(m), place, place, c_ss.at[m - 1], c_rs.at[it, m - 1])

    def o_copy(it):
        return send_ves(
            1, joined.at[it, pl.ds(n_chunks, n_chunks)], joined.at[it, pl.ds(0, n_chunks)], o_ss.at[0], o_rs.at[it]
        )

    barrier = pltpu.get_barrier_semaphore()

    def greet_ves(k, carry):
        pl.semaphore_signal(barrier, 1, device_id={"ves": ves_at(k)}, device_id_type=MESH)
        return carry

    def greet_near(m, carry):
        pl.semaphore_signal(barrier, 1, device_id={"tis": tis_near(m)}, device_id_type=MESH)
        return carry

    def greet_along(k, carry):
        pl.semaphore_signal(barrier, 1, device_id={"tis": tis_along(k)}, device_id_type=MESH)
        return carry

    lax.fori_loop(1, n_ves, greet_ves, 0)
    lax.fori_loop(1, 4, greet_near, 0)
    lax.fori_loop(1, n_z, greet_along, 0)

    solute = lax.broadcasted_iota(jnp.int32, (8, LANES), 0)
    lane = lax.broadcasted_iota(jnp.int32, (8, LANES), 1)

    def column(ref):
        out = jnp.zeros((8, LANES), f32)
        for s in range(8):
            out = jnp.where(solute == s, ref[s], out)
        return out

    half = column(half_ref)[:, :1]
    diff = column(diff_ref)[:, :1]
    base[...] = column(base_ref)

    feat[...] = jnp.zeros_like(feat)
    square = jnp.zeros((1, pts), f32)
    for d in range(3):
        p = point_ref[d : d + 1, :] - 0.5
        square = square + p * p
        for a, piece in enumerate(pieces(p)):
            for b in range(3):
                row = 9 * d + 3 * a + b
                feat[row : row + 1, :pts] = piece
    for a, piece in enumerate(pieces(square)):
        feat[27 + a : 28 + a, :pts] = piece
        feat[30 + a : 31 + a, :pts] = jnp.ones((1, pts), f32)

    def turn(i, carry):
        point_feat[at(i, LANES), :] = feat[:, at(i, LANES)].T.astype(bf16)
        return carry

    lax.fori_loop(0, pts // LANES, turn, 0)

    square = radius_ref[...] * radius_ref[...]
    for d in range(3):
        s = seg_ref[d : d + 1, :] - 0.5
        square = square + s * s
        for b, piece in enumerate(pieces(s)):
            for a in range(3):
                row = 9 * d + 3 * a + b
                feat[row : row + 1, :segs] = -2.0 * piece
    for a, piece in enumerate(pieces(square)):
        feat[27 + a : 28 + a, :segs] = jnp.ones((1, segs), f32)
        feat[30 + a : 31 + a, :segs] = piece
    seg_feat[...] = feat[:, :segs].astype(bf16)

    table = table_ref[...]
    for i in range(pts // LANES):
        cell = jnp.broadcast_to(cell_ref[:, i * LANES : (i + 1) * LANES], (8, LANES))
        rates[:, i * LANES : (i + 1) * LANES] = jnp.take_along_axis(table, cell, axis=1)

    total = jnp.zeros((8, LANES), f32)
    for i in range(n_chunks):
        cols = slice(i * LANES, (i + 1) * LANES)
        own, held = sources_ref[:, cols], contents_ref[:, cols]
        src[0, i // per_q, i % per_q] = own
        cont[i] = held
        joined[0, n_chunks + i] = held - own * flow_ref[:, cols]
        total = total + own
    for k in range(n_ves):
        t_send[k, :, chunk:] = total

    def build(k, carry):
        of = ves_at(k % n_ves)
        rows = at(of, chunk)
        block = lax.rsqrt(dot(point_feat[rows, :], seg_feat[...])).astype(bf16)
        tile[rows, :] = block
        t_send[k % n_ves, :, :chunk] = dot_nt(sources_ref[...].astype(bf16), block)

        @pl.when(k == 1)
        def _():
            pl.semaphore_wait(barrier, n_ves - 1 + 3 + n_z - 1)
            o_copy(0).start()

        @pl.when(k < n_ves)
        def _():
            t_copy(0, k).start()

        return carry

    lax.fori_loop(1, n_ves + 1, build, 0)

    def sweep(it, carry):
        o_copy(it).wait()

        def gather(c, carry):
            cols = at(c, LANES)
            parent = jnp.broadcast_to(parent_ref[:, cols], (8, LANES))
            root = parent == v * segs + c * LANES + lane
            offset = parent - (v * segs - segs) - c * LANES
            which, place = offset >> 7, offset & (LANES - 1)
            found = jnp.zeros((8, LANES), f32)
            for h in range(n_chunks + 1):
                found = jnp.where(which == h, jnp.take_along_axis(joined[it, c + h], place, axis=1), found)
            cont[c] = jnp.where(root, inflow_ref[:, cols], found)
            return carry

        lax.fori_loop(0, n_chunks, gather, 0)

        summed = t_send[0]
        for k in range(1, n_ves):
            t_copy(it, k).wait()
            summed = summed + t_recv[it, k - 1]
        level[it, v] = base[:, :1] + summed[:, :chunk] / (diff * total_segs)

        def share(k, carry):
            l_copy(it, k, v).start()
            return carry

        lax.fori_loop(1, n_ves, share, 0)
        sink_sum[...] = jnp.zeros_like(sink_sum)

        def sink_of(k):
            of = (v + n_ves - k) % n_ves

            @pl.when(k > 0)
            def _():
                l_copy(it, k, of).wait()

            now = level[it, of]
            value = rates[:, at(of, chunk)] * now / (jnp.abs(now) + half)
            sink[k] = value
            part = value[:, :LANES]
            for i in range(1, chunk // LANES):
                part = part + value[:, i * LANES : (i + 1) * LANES]
            sink_sum[...] += part
            return of

        wall[...] = jnp.zeros_like(wall)

        def early(k, carry):
            of = sink_of(k)
            wall[...] += dot(sink[k].astype(bf16), tile[at(of, chunk), :])
            return carry

        def late(k, carry):
            sink_of(k)
            return carry

        lax.fori_loop(0, n_ves // 2, early, 0)
        lax.fori_loop(n_ves // 2, n_ves, late, 0)

        def finish(i, carry):
            m = 3 - i
            cols = at(quarter_of(m), quarter)
            part = wall[:, cols]
            for k in range(n_ves // 2, n_ves):
                of = (v + n_ves - k) % n_ves
                part = part + dot(sink[k].astype(bf16), tile[at(of, chunk), cols])
            a_send[m, :, :quarter] = part
            a_send[m, :, quarter:] = sink_sum[...]

            @pl.when(m > 0)
            def _():
                a_copy(it, m).start()

            return carry

        lax.fori_loop(0, 4, finish, 0)
        own = a_send[0]
        for m in range(1, 4):
            a_copy(it, m).wait()
            own = own + a_recv[it, m - 1]
        for i in range(n_z):
            b_send[i, :, :LANES] = own[:, i * LANES : (i + 1) * LANES]
            b_send[i, :, LANES:] = own[:, quarter:]

        def spread(k, carry):
            b_copy(it, k).start()
            return carry

        lax.fori_loop(1, n_z, spread, 0)
        own = b_send[z]
        for k in range(1, n_z):
            b_copy(it, k).wait()
            own = own + b_recv[it, k - 1]
        q = quarter_of(0)
        cols = at(q * per_q + z, LANES)
        wall_field = own[:, :LANES] / (diff * total_pts)
        src[it + 1, q, z] = RELAX * src[it, q, z] + RELAX * cond_ref[:, cols] * (cont[q * per_q + z] - wall_field)

        def along(k, carry):
            z_copy(it, k, z).start()
            return carry

        lax.fori_loop(1, n_z, along, 0)
        source_total = jnp.sum(summed[:, chunk:], axis=1, keepdims=True)
        sink_total = jnp.sum(own[:, LANES:], axis=1, keepdims=True)
        base[...] += BALANCE * (source_total / total_segs - sink_total / total_pts)
        for k in range(1, n_z):
            z_copy(it, k, (z + n_z - k) % n_z).wait()

        def beside(m, carry):
            c_copy(it, m, q).start()
            return carry

        lax.fori_loop(1, 4, beside, 0)

        def source_block(of):
            return jnp.concatenate([src[it + 1, of, i] for i in range(per_q)], axis=1).astype(bf16)

        @pl.when(it < ITERS - 1)
        def _():
            rows_at_once = pts // 4

            def first(i, carry):
                rows = at(i, rows_at_once)
                t_sum[:, rows] = dot_nt(source_block(q), tile[rows, at(q, quarter)])
                return carry

            lax.fori_loop(0, 4, first, 0)

            def middle(m, carry):
                of = quarter_of(m)
                c_copy(it, m, of).wait()

                def some(i, carry):
                    rows = at(i, rows_at_once)
                    t_sum[:, rows] += dot_nt(source_block(of), tile[rows, at(of, quarter)])
                    return carry

                return lax.fori_loop(0, 4, some, carry)

            lax.fori_loop(1, 3, middle, 0)
            of = quarter_of(3)
            c_copy(it, 3, of).wait()

            total = jnp.zeros((8, LANES), f32)
            for i in range(n_chunks):
                cols = slice(i * LANES, (i + 1) * LANES)
                now = src[it + 1, i // per_q, i % per_q]
                joined[it + 1, n_chunks + i] = cont[i] - now * flow_ref[:, cols]
                total = total + now
            for k in range(n_ves):
                t_send[k, :, chunk:] = total
            o_copy(it + 1).start()

            def last(k, carry):
                rows = at(ves_at(k % n_ves), chunk)
                t_send[k % n_ves, :, :chunk] = t_sum[:, rows] + dot_nt(
                    source_block(of), tile[rows, at(of, quarter)]
                )

                @pl.when(k < n_ves)
                def _():
                    t_copy(it + 1, k).start()

                return carry

            lax.fori_loop(1, n_ves + 1, last, 0)

        @pl.when(it == ITERS - 1)
        def _():
            for i in range(n_ves):
                level_out[:, i * chunk : (i + 1) * chunk] = level[it, i]
            for i in range(n_chunks):
                contents_out[:, i * LANES : (i + 1) * LANES] = cont[i]
            for m in range(1, 4):
                c_copy(it, m, quarter_of(m)).wait()
            for i in range(n_chunks):
                sources_out[:, i * LANES : (i + 1) * LANES] = src[it + 1, i // per_q, i % per_q]

        return carry

    lax.fori_loop(0, ITERS, sweep, 0)


def body(
    point_xyz,
    point_cell,
    seg_xyz,
    seg_radius,
    conductance,
    flow_inv,
    parent,
    inflow,
    rate_table,
    half_sat,
    diffusivity,
    base_level,
    sources,
    contents,
):
    n_ves = lax.axis_size("ves")
    n_z = lax.axis_size("tis") // 4
    pts, segs = point_xyz.shape[1], seg_xyz.shape[1]
    chunk, quarter, n_chunks = pts // n_ves, segs // 4, segs // LANES
    f32, bf16 = jnp.float32, jnp.bfloat16
    vmem = pl.BlockSpec(memory_space=pltpu.VMEM)
    smem = pl.BlockSpec(memory_space=pltpu.SMEM)
    sem = pltpu.SemaphoreType.DMA
    line = lambda x: x.reshape(1, -1)
    return pl.pallas_call(
        functools.partial(kernel, n_ves, n_z, pts, segs),
        out_shape=(
            jax.ShapeDtypeStruct((8, pts), f32),
            jax.ShapeDtypeStruct((8, segs), f32),
            jax.ShapeDtypeStruct((8, segs), f32),
        ),
        in_specs=[vmem] * 9 + [smem] * 3 + [vmem] * 2,
        out_specs=(vmem, vmem, vmem),
        scratch_shapes=[
            pltpu.VMEM((pts, segs), bf16),
            pltpu.VMEM((pts, FEATURES), bf16),
            pltpu.VMEM((FEATURES, segs), bf16),
            pltpu.VMEM((FEATURES, max(pts, segs)), f32),
            pltpu.VMEM((8, pts), f32),
            pltpu.VMEM((8, LANES), f32),
            pltpu.VMEM((8, pts), f32),
            pltpu.VMEM((n_ves, 8, chunk + LANES), f32),
            pltpu.VMEM((ITERS, n_ves - 1, 8, chunk + LANES), f32),
            pltpu.VMEM((ITERS, n_ves, 8, chunk), f32),
            pltpu.VMEM((n_ves, 8, chunk), f32),
            pltpu.VMEM((8, LANES), f32),
            pltpu.VMEM((8, segs), f32),
            pltpu.VMEM((4, 8, quarter + LANES), f32),
            pltpu.VMEM((ITERS, 3, 8, quarter + LANES), f32),
            pltpu.VMEM((n_z, 8, 2 * LANES), f32),
            pltpu.VMEM((ITERS, n_z - 1, 8, 2 * LANES), f32),
            pltpu.VMEM((ITERS + 1, 4, n_z, 8, LANES), f32),
            pltpu.VMEM((n_chunks, 8, LANES), f32),
            pltpu.VMEM((ITERS, 2 * n_chunks, 8, LANES), f32),
            sem((n_ves - 1,)),
            sem((ITERS, n_ves - 1)),
            sem((n_ves - 1,)),
            sem((ITERS, n_ves - 1)),
            sem((3,)),
            sem((ITERS, 3)),
            sem((n_z - 1,)),
            sem((ITERS, n_z - 1)),
            sem((n_z - 1,)),
            sem((ITERS, n_z - 1)),
            sem((3,)),
            sem((ITERS, 3)),
            sem((1,)),
            sem((ITERS,)),
        ],
        compiler_params=pltpu.CompilerParams(
            collective_id=0, has_side_effects=True, vmem_limit_bytes=60 * 2**20
        ),
        name="exchange",
    )(
        point_xyz,
        line(point_cell),
        seg_xyz,
        line(seg_radius),
        line(conductance),
        line(flow_inv),
        line(parent),
        inflow,
        rate_table,
        half_sat,
        diffusivity,
        base_level,
        sources,
        contents,
    )


def solution(mesh):
    return jax.shard_map(
        body,
        mesh=mesh,
        in_specs=(
            P(None, "tis"),
            P("tis"),
            P(None, "ves"),
            P("ves"),
            P("ves"),
            P("ves"),
            P("ves"),
            P(None, "ves"),
            P(),
            P(),
            P(),
            P(),
            P(None, "ves"),
            P(None, "ves"),
        ),
        out_specs=(P(None, "tis"), P(None, "ves"), P(None, "ves")),
        check_vma=False,
    )
```

```python
import functools

import jax
import jax.numpy as jnp
from jax import lax
from jax.experimental import pallas as pl
from jax.experimental.pallas import tpu as pltpu
from jax.sharding import PartitionSpec as P

ITERS = 3
RELAX = 0.5
BALANCE = 0.5
LANES = 128
FEATURES = 48
MESH = pl.DeviceIdType.MESH


def pieces(x):
    high = x.astype(jnp.bfloat16).astype(jnp.float32)
    rest = x - high
    middle = rest.astype(jnp.bfloat16).astype(jnp.float32)
    return high, middle, (rest - middle).astype(jnp.bfloat16).astype(jnp.float32)


def dot(a, b):
    return jnp.dot(a, b, preferred_element_type=jnp.float32)


def dot_nt(a, b):
    return lax.dot_general(a, b, (((1,), (1,)), ((), ())), preferred_element_type=jnp.float32)


def at(i, size):
    return pl.ds(pl.multiple_of(i * size, size), size)


def kernel(
    n_ves,
    n_z,
    pts,
    segs,
    point_ref,
    cell_ref,
    seg_ref,
    radius_ref,
    cond_ref,
    flow_ref,
    parent_ref,
    inflow_ref,
    table_ref,
    half_ref,
    diff_ref,
    base_ref,
    sources_ref,
    contents_ref,
    level_out,
    sources_out,
    contents_out,
    tile,
    point_feat,
    seg_feat,
    feat,
    feat_seg,
    rates,
    base,
    t_sum,
    t_send,
    t_recv,
    level,
    sink,
    sink_sum,
    wall,
    a_send,
    a_recv,
    b_send,
    b_recv,
    src,
    cont,
    joined,
    t_ss,
    t_rs,
    l_ss,
    l_rs,
    a_ss,
    a_rs,
    b_ss,
    b_rs,
    z_ss,
    z_rs,
    c_ss,
    c_rs,
    o_ss,
    o_rs,
):
    f32, bf16 = jnp.float32, jnp.bfloat16
    n_tis = 4 * n_z
    chunk = pts // n_ves
    quarter = segs // 4
    n_chunks = segs // LANES
    per_q = n_z
    total_pts = pts * n_tis
    total_segs = segs * n_ves
    t, v = lax.axis_index("tis"), lax.axis_index("ves")
    y, z, core = t // (2 * n_z), (t // 2) % n_z, t % 2

    def quarter_of(core, y):
        return core % 2 * 2 + y % 2

    def tis_at(k):
        return ((y + k // n_z) % 2) * (2 * n_z) + ((z + k % n_z) % n_z) * 2 + core

    other_core = y * (2 * n_z) + z * 2 + (core + 1) % 2

    n_x = n_ves // 2
    n_pairs = n_z // 2
    v_y, v_x = v // n_x, v % n_x

    def ves_at(k):
        return ((v_y + k // n_x) % 2) * n_x + (v_x + k % n_x) % n_x

    def ves_from(k):
        return ((v_y + k // n_x) % 2) * n_x + (v_x + n_x - k % n_x) % n_x

    far_first = sorted(range(1, 2 * n_z), key=lambda k: -(k // n_z) - min(k % n_z, n_z - k % n_z))
    near_first = sorted(range(n_pairs), key=lambda k: min(k, n_pairs - k))

    def send_ves(k, a, b, s, r):
        return pltpu.make_async_remote_copy(
            src_ref=a, dst_ref=b, send_sem=s, recv_sem=r, device_id={"ves": ves_at(k)}, device_id_type=MESH
        )

    def send_tis(to, a, b, s, r):
        return pltpu.make_async_remote_copy(
            src_ref=a, dst_ref=b, send_sem=s, recv_sem=r, device_id={"tis": to}, device_id_type=MESH
        )

    def t_copy(it, k):
        return send_ves(k, t_send.at[k], t_recv.at[it, k - 1], t_ss.at[k - 1], t_rs.at[it, k - 1])

    def l_copy(it, k, of):
        return send_ves(k, level.at[it, of], level.at[it, of], l_ss.at[k - 1], l_rs.at[it, k - 1])

    def a_copy(it, i):
        return send_tis(other_core, a_send.at[i], a_recv.at[it, i], a_ss.at[i], a_rs.at[it, i])

    def b_copy(it, k):
        block = b_send.at[(y + k // n_z) % 2, (z + k % n_z) % n_z]
        return send_tis(tis_at(k), block, b_recv.at[it, k - 1], b_ss.at[k - 1], b_rs.at[it, k - 1])

    def z_copy(it, k, q, of):
        place = src.at[it + 1, q, of]
        return send_tis(tis_at(k), place, place, z_ss.at[k - 1], z_rs.at[it, k - 1])

    def c_copy(it, i, q):
        place = src.at[it + 1, q]
        return send_tis(other_core, place, place, c_ss.at[i], c_rs.at[it, i])

    def o_copy(it):
        return pltpu.make_async_remote_copy(
            src_ref=joined.at[it, pl.ds(n_chunks, n_chunks)],
            dst_ref=joined.at[it, pl.ds(0, n_chunks)],
            send_sem=o_ss.at[0],
            recv_sem=o_rs.at[it],
            device_id={"ves": (v + 1) % n_ves},
            device_id_type=MESH,
        )

    barrier = pltpu.get_barrier_semaphore()

    def greet_ves(k, carry):
        pl.semaphore_signal(barrier, 1, device_id={"ves": ves_at(k)}, device_id_type=MESH)
        return carry

    def greet_tis(k, carry):
        pl.semaphore_signal(barrier, 1, device_id={"tis": tis_at(k)}, device_id_type=MESH)
        return carry

    lax.fori_loop(1, n_ves, greet_ves, 0)
    lax.fori_loop(1, 2 * n_z, greet_tis, 0)
    pl.semaphore_signal(barrier, 1, device_id={"tis": other_core}, device_id_type=MESH)

    solute = lax.broadcasted_iota(jnp.int32, (8, LANES), 0)
    lane = lax.broadcasted_iota(jnp.int32, (8, LANES), 1)

    def column(ref):
        out = jnp.zeros((8, LANES), f32)
        for s in range(8):
            out = jnp.where(solute == s, ref[s], out)
        return out

    half = column(half_ref)[:, :1]
    diff = column(diff_ref)[:, :1]
    base[...] = column(base_ref)

    feat[...] = jnp.zeros_like(feat)
    feat_seg[...] = jnp.zeros_like(feat_seg)
    square = jnp.zeros((1, pts), f32)
    for d in range(3):
        p = point_ref[d : d + 1, :] - 0.5
        square = square + p * p
        for a, piece in enumerate(pieces(p)):
            for b in range(3):
                row = 9 * d + 3 * a + b
                feat[row : row + 1, :] = piece
    for a, piece in enumerate(pieces(square)):
        feat[27 + a : 28 + a, :] = piece
        feat[30 + a : 31 + a, :] = jnp.ones((1, pts), f32)

    def turn(k):
        for i in range(chunk // LANES):
            cols = at(ves_at(k) * (chunk // LANES) + i, LANES)
            point_feat[cols, :] = feat[:, cols].T.astype(bf16)

    turn(n_ves - 1)

    square = radius_ref[...] * radius_ref[...]
    for d in range(3):
        s = seg_ref[d : d + 1, :] - 0.5
        square = square + s * s
        for b, piece in enumerate(pieces(s)):
            for a in range(3):
                row = 9 * d + 3 * a + b
                feat_seg[row : row + 1, :] = -2.0 * piece
    for a, piece in enumerate(pieces(square)):
        feat_seg[27 + a : 28 + a, :] = jnp.ones((1, segs), f32)
        feat_seg[30 + a : 31 + a, :] = piece
    seg_feat[...] = feat_seg[...].astype(bf16)

    table = table_ref[...]
    for i in range(pts // LANES):
        cell = jnp.broadcast_to(cell_ref[:, i * LANES : (i + 1) * LANES], (8, LANES))
        rates[:, i * LANES : (i + 1) * LANES] = jnp.take_along_axis(table, cell, axis=1)

    total = jnp.zeros((8, LANES), f32)
    for i in range(n_chunks):
        cols = slice(i * LANES, (i + 1) * LANES)
        own, held = sources_ref[:, cols], contents_ref[:, cols]
        src[0, i // per_q, i % per_q] = own
        cont[i] = held
        joined[0, n_chunks + i] = held - own * flow_ref[:, cols]
        total = total + own
    for k in range(n_ves):
        t_send[k, :, chunk:] = total

    def build(i, carry):
        k = n_ves - 1 - i
        rows = at(ves_at(k), chunk)
        turn((k + n_ves - 1) % n_ves)
        block = lax.rsqrt(dot(point_feat[rows, :], seg_feat[...])).astype(bf16)
        tile[rows, :] = block
        t_send[k, :, :chunk] = dot_nt(sources_ref[...].astype(bf16), block)

        @pl.when(i == 0)
        def _():
            pl.semaphore_wait(barrier, n_ves - 1 + 2 * n_z)

        @pl.when(k > 0)
        def _():
            t_copy(0, k).start()

        return carry

    lax.fori_loop(0, n_ves, build, 0)

    def sweep(it, carry):
        summed = t_send[0]
        for k in range(1, n_ves):
            t_copy(it, k).wait()
            summed = summed + t_recv[it, k - 1]
        level[it, v] = base[:, :1] + summed[:, :chunk] / (diff * total_segs)

        def share(i, carry):
            l_copy(it, n_ves - 1 - i, v).start()
            return carry

        lax.fori_loop(0, n_ves - 1, share, 0)
        o_copy(it).start()
        sink_sum[...] = jnp.zeros_like(sink_sum)

        def sink_of(k):
            of = ves_from(k)

            @pl.when(k > 0)
            def _():
                l_copy(it, k, of).wait()

            now = level[it, of]
            value = rates[:, at(of, chunk)] * now / (jnp.abs(now) + half)
            sink[k] = value
            part = value[:, :LANES]
            for i in range(1, chunk // LANES):
                part = part + value[:, i * LANES : (i + 1) * LANES]
            sink_sum[...] += part
            return of

        wall[...] = jnp.zeros_like(wall)

        def early(k, carry):
            of = sink_of(k)
            wall[...] += dot(sink[k].astype(bf16), tile[at(of, chunk), :])
            return carry

        def late(k, carry):
            sink_of(k)
            return carry

        lax.fori_loop(0, n_ves // 2, early, 0)
        lax.fori_loop(n_ves // 2, n_ves, late, 0)

        sums = jnp.sum(sink_sum[...], axis=1, keepdims=True)
        sink_row = jnp.sum(jnp.where(solute == lane, sums, 0.0), axis=0, keepdims=True)
        for i in range(4):
            a_send[i, :, quarter:] = jnp.broadcast_to(sink_row, (8, LANES))

        def finish(i, carry):
            cols = at(quarter_of(core + 1 + i // 2, i), quarter)
            part = wall[:, cols]
            for k in range(n_ves // 2, n_ves):
                of = ves_from(k)
                part = part + dot(sink[k].astype(bf16), tile[at(of, chunk), cols])
            a_send[i, :, :quarter] = part

            @pl.when(i < 2)
            def _():
                a_copy(it, i).start()

            return carry

        lax.fori_loop(0, 4, finish, 0)
        for h in range(2):
            a_copy(it, h).wait()
            own = a_send[2 + h] + a_recv[it, h]
            for i in range(n_z):
                b_send[h, i, :8, :] = own[:, i * LANES : (i + 1) * LANES]
                b_send[h, i, 8:, :] = own[:1, quarter:]

        for k in far_first:
            b_copy(it, k).start()

        o_copy(it).wait()

        def gather(c, carry):
            cols = at(c, LANES)
            parent = jnp.broadcast_to(parent_ref[:, cols], (8, LANES))
            root = parent == v * segs + c * LANES + lane
            offset = parent - (v * segs - segs) - c * LANES
            which, place = offset >> 7, offset & (LANES - 1)
            found = jnp.zeros((8, LANES), f32)
            for h in range(n_chunks + 1):
                found = jnp.where(which == h, jnp.take_along_axis(joined[it, c + h], place, axis=1), found)
            cont[c] = jnp.where(root, inflow_ref[:, cols], found)
            return carry

        lax.fori_loop(0, n_chunks, gather, 0)

        own = b_send[y, z]
        for k in range(1, 2 * n_z):
            b_copy(it, k).wait()
            own = own + b_recv[it, k - 1]
        q = quarter_of(core, y)
        cols = at(q * per_q + z, LANES)
        wall_field = own[:8] / (diff * total_pts)
        src[it + 1, q, z] = RELAX * src[it, q, z] + RELAX * cond_ref[:, cols] * (cont[q * per_q + z] - wall_field)
        for k in far_first:
            z_copy(it, k, q, z).start()
        source_total = jnp.sum(summed[:, chunk:], axis=1, keepdims=True)
        sink_total = jnp.sum(jnp.where(solute == lane, own[8:], 0.0), axis=1, keepdims=True)
        base[...] += BALANCE * (source_total / total_segs - sink_total / total_pts)

        def source_block(of):
            return jnp.concatenate([src[it + 1, of, i] for i in range(per_q)], axis=1).astype(bf16)

        for step in range(2 * n_pairs):
            from_y = (y + step // n_pairs) % 2
            pair = (z // 2 + near_first[step % n_pairs]) % n_pairs
            q = quarter_of(core, from_y)
            for e in range(2):
                of = pair * 2 + e
                k = (step // n_pairs) * n_z + (z + n_z - of) % n_z

                @pl.when(k > 0)
                def _():
                    z_copy(it, k, q, of).wait()

            if step % n_pairs == n_pairs - 1:
                c_copy(it, step // n_pairs, q).start()

            @pl.when(it < ITERS - 1)
            def _():
                two = jnp.concatenate([src[it + 1, q, pair * 2], src[it + 1, q, pair * 2 + 1]], axis=1).astype(bf16)
                part = dot_nt(two, tile[:, pl.ds(pl.multiple_of(q * quarter + pair * 2 * LANES, LANES), 2 * LANES)])
                if step == 0:
                    t_sum[...] = part
                else:
                    t_sum[...] += part

        @pl.when(it < ITERS - 1)
        def _():
            of = quarter_of(core + 1, y)
            c_copy(it, 0, of).wait()
            t_sum[...] += dot_nt(source_block(of), tile[:, at(of, quarter)])
            of = quarter_of(core + 1, y + 1)
            c_copy(it, 1, of).wait()

            total = jnp.zeros((8, LANES), f32)
            for i in range(n_chunks):
                cols = slice(i * LANES, (i + 1) * LANES)
                now = src[it + 1, i // per_q, i % per_q]
                joined[it + 1, n_chunks + i] = cont[i] - now * flow_ref[:, cols]
                total = total + now
            for k in range(n_ves):
                t_send[k, :, chunk:] = total

            def last(i, carry):
                k = n_ves - 1 - i
                rows = at(ves_at(k), chunk)
                t_send[k, :, :chunk] = t_sum[:, rows] + dot_nt(
                    source_block(of), tile[rows, at(of, quarter)]
                )

                @pl.when(k > 0)
                def _():
                    t_copy(it + 1, k).start()

                return carry

            lax.fori_loop(0, n_ves, last, 0)

        @pl.when(it == ITERS - 1)
        def _():
            for i in range(n_ves):
                level_out[:, i * chunk : (i + 1) * chunk] = level[it, i]
            for i in range(n_chunks):
                contents_out[:, i * LANES : (i + 1) * LANES] = cont[i]
            for i in range(2):
                c_copy(it, i, quarter_of(core + 1, y + i)).wait()
            for i in range(n_chunks):
                sources_out[:, i * LANES : (i + 1) * LANES] = src[it + 1, i // per_q, i % per_q]

        return carry

    lax.fori_loop(0, ITERS, sweep, 0)


def hand_over(a, b, c, a_out, b_out, c_out):
    a_out[...] = a[...]
    b_out[...] = b[...]
    c_out[...] = c[...]


def body(
    point_xyz,
    point_cell,
    seg_xyz,
    seg_radius,
    conductance,
    flow_inv,
    parent,
    inflow,
    rate_table,
    half_sat,
    diffusivity,
    base_level,
    sources,
    contents,
):
    n_ves = lax.axis_size("ves")
    n_z = lax.axis_size("tis") // 4
    pts, segs = point_xyz.shape[1], seg_xyz.shape[1]
    chunk, quarter, n_chunks = pts // n_ves, segs // 4, segs // LANES
    f32, bf16 = jnp.float32, jnp.bfloat16
    vmem = pl.BlockSpec(memory_space=pltpu.VMEM)
    smem = pl.BlockSpec(memory_space=pltpu.SMEM)
    sem = pltpu.SemaphoreType.DMA
    line = lambda x: x.reshape(1, -1)
    out = pl.pallas_call(
        functools.partial(kernel, n_ves, n_z, pts, segs),
        out_shape=(
            jax.ShapeDtypeStruct((8, pts), f32),
            jax.ShapeDtypeStruct((8, segs), f32),
            jax.ShapeDtypeStruct((8, segs), f32),
        ),
        in_specs=[vmem] * 9 + [smem] * 3 + [vmem] * 2,
        out_specs=(vmem, vmem, vmem),
        scratch_shapes=[
            pltpu.VMEM((pts, segs), bf16),
            pltpu.VMEM((pts, FEATURES), bf16),
            pltpu.VMEM((FEATURES, segs), bf16),
            pltpu.VMEM((FEATURES, pts), f32),
            pltpu.VMEM((FEATURES, segs), f32),
            pltpu.VMEM((8, pts), f32),
            pltpu.VMEM((8, LANES), f32),
            pltpu.VMEM((8, pts), f32),
            pltpu.VMEM((n_ves, 8, chunk + LANES), f32),
            pltpu.VMEM((ITERS, n_ves - 1, 8, chunk + LANES), f32),
            pltpu.VMEM((ITERS, n_ves, 8, chunk), f32),
            pltpu.VMEM((n_ves, 8, chunk), f32),
            pltpu.VMEM((8, LANES), f32),
            pltpu.VMEM((8, segs), f32),
            pltpu.VMEM((4, 8, quarter + LANES), f32),
            pltpu.VMEM((ITERS, 2, 8, quarter + LANES), f32),
            pltpu.VMEM((2, n_z, 9, LANES), f32),
            pltpu.VMEM((ITERS, 2 * n_z - 1, 9, LANES), f32),
            pltpu.VMEM((ITERS + 1, 4, n_z, 8, LANES), f32),
            pltpu.VMEM((n_chunks, 8, LANES), f32),
            pltpu.VMEM((ITERS, 2 * n_chunks, 8, LANES), f32),
            sem((n_ves - 1,)),
            sem((ITERS, n_ves - 1)),
            sem((n_ves - 1,)),
            sem((ITERS, n_ves - 1)),
            sem((2,)),
            sem((ITERS, 2)),
            sem((2 * n_z - 1,)),
            sem((ITERS, 2 * n_z - 1)),
            sem((2 * n_z - 1,)),
            sem((ITERS, 2 * n_z - 1)),
            sem((2,)),
            sem((ITERS, 2)),
            sem((1,)),
            sem((ITERS,)),
        ],
        compiler_params=pltpu.CompilerParams(
            collective_id=0, has_side_effects=True, vmem_limit_bytes=60 * 2**20
        ),
        name="exchange",
    )(
        point_xyz,
        line(point_cell),
        seg_xyz,
        line(seg_radius),
        line(conductance),
        line(flow_inv),
        line(parent),
        inflow,
        rate_table,
        half_sat,
        diffusivity,
        base_level,
        sources,
        contents,
    )
    return pl.pallas_call(
        hand_over,
        out_shape=tuple(jax.ShapeDtypeStruct(x.shape, f32) for x in out),
        in_specs=[vmem] * 3,
        out_specs=(vmem,) * 3,
        name="hand_over",
    )(*out)


def solution(mesh):
    return jax.shard_map(
        body,
        mesh=mesh,
        in_specs=(
            P(None, "tis"),
            P("tis"),
            P(None, "ves"),
            P("ves"),
            P("ves"),
            P("ves"),
            P("ves"),
            P(None, "ves"),
            P(),
            P(),
            P(),
            P(),
            P(None, "ves"),
            P(None, "ves"),
        ),
        out_specs=(P(None, "tis"), P(None, "ves"), P(None, "ves")),
        check_vma=False,
    )
```

```python
import functools

import jax
import jax.numpy as jnp
from jax import lax
from jax.experimental import pallas as pl
from jax.experimental.pallas import tpu as pltpu
from jax.sharding import PartitionSpec as P

ITERS = 3
RELAX = 0.5
BALANCE = 0.5
LANES = 128
FEATURES = 80
MESH = pl.DeviceIdType.MESH


def pieces(x):
    high = x.astype(jnp.bfloat16).astype(jnp.float32)
    rest = x - high
    middle = rest.astype(jnp.bfloat16).astype(jnp.float32)
    return high, middle, (rest - middle).astype(jnp.bfloat16).astype(jnp.float32)


def dot(a, b):
    return jnp.dot(a, b, preferred_element_type=jnp.float32)


def dot_nt(a, b):
    return lax.dot_general(a, b, (((1,), (1,)), ((), ())), preferred_element_type=jnp.float32)


def at(i, size):
    return pl.ds(pl.multiple_of(i * size, size), size)


def kernel(
    n_ves,
    n_z,
    pts,
    segs,
    point_ref,
    cell_ref,
    seg_ref,
    radius_ref,
    cond_ref,
    flow_ref,
    parent_ref,
    inflow_ref,
    table_ref,
    half_ref,
    diff_ref,
    base_ref,
    sources_ref,
    contents_ref,
    level_out,
    sources_out,
    contents_out,
    tile,
    point_feat,
    seg_feat,
    feat,
    feat_seg,
    rates,
    base,
    t_sum,
    t_send,
    t_recv,
    level,
    sink,
    sink_sum,
    wall,
    a_send,
    a_recv,
    b_send,
    b_recv,
    src,
    cont,
    joined,
    t_ss,
    t_rs,
    l_ss,
    l_rs,
    a_ss,
    a_rs,
    b_ss,
    b_rs,
    z_ss,
    z_rs,
    c_ss,
    c_rs,
    o_ss,
    o_rs,
):
    f32, bf16 = jnp.float32, jnp.bfloat16
    n_tis = 4 * n_z
    chunk = pts // n_ves
    quarter = segs // 4
    n_chunks = segs // LANES
    per_q = n_z
    total_pts = pts * n_tis
    total_segs = segs * n_ves
    t, v = lax.axis_index("tis"), lax.axis_index("ves")
    y, z, core = t // (2 * n_z), (t // 2) % n_z, t % 2

    def quarter_of(core, y):
        return core % 2 * 2 + y % 2

    def tis_at(k):
        return ((y + k // n_z) % 2) * (2 * n_z) + ((z + k % n_z) % n_z) * 2 + core

    other_core = y * (2 * n_z) + z * 2 + (core + 1) % 2

    n_x = n_ves // 2
    n_early = n_ves - max(1, n_ves * 3 // 8)
    n_pairs = n_z // 2
    v_y, v_x = v // n_x, v % n_x

    def ves_at(k):
        return ((v_y + k // n_x) % 2) * n_x + (v_x + k % n_x) % n_x

    def ves_from(k):
        return ((v_y + k // n_x) % 2) * n_x + (v_x + n_x - k % n_x) % n_x

    far_first = sorted(range(1, 2 * n_z), key=lambda k: -(k // n_z) - min(k % n_z, n_z - k % n_z))
    near_first = sorted(range(n_pairs), key=lambda k: min(k, n_pairs - k))

    def send_ves(k, a, b, s, r):
        return pltpu.make_async_remote_copy(
            src_ref=a, dst_ref=b, send_sem=s, recv_sem=r, device_id={"ves": ves_at(k)}, device_id_type=MESH
        )

    def send_tis(to, a, b, s, r):
        return pltpu.make_async_remote_copy(
            src_ref=a, dst_ref=b, send_sem=s, recv_sem=r, device_id={"tis": to}, device_id_type=MESH
        )

    def t_copy(it, k):
        return send_ves(k, t_send.at[k], t_recv.at[it, k - 1], t_ss.at[k - 1], t_rs.at[it, k - 1])

    def l_copy(it, k, of):
        return send_ves(k, level.at[it, of], level.at[it, of], l_ss.at[k - 1], l_rs.at[it, k - 1])

    def a_copy(it, i):
        return send_tis(other_core, a_send.at[i], a_recv.at[it, i], a_ss.at[i], a_rs.at[it, i])

    def b_copy(it, k):
        block = b_send.at[(y + k // n_z) % 2, (z + k % n_z) % n_z]
        return send_tis(tis_at(k), block, b_recv.at[it, k - 1], b_ss.at[k - 1], b_rs.at[it, k - 1])

    def z_copy(it, k, q, of):
        place = src.at[it + 1, q, of]
        return send_tis(tis_at(k), place, place, z_ss.at[k - 1], z_rs.at[it, k - 1])

    def c_copy(it, i, q):
        place = src.at[it + 1, q]
        return send_tis(other_core, place, place, c_ss.at[i], c_rs.at[it, i])

    def o_copy(it):
        return pltpu.make_async_remote_copy(
            src_ref=joined.at[it, pl.ds(n_chunks, n_chunks)],
            dst_ref=joined.at[it, pl.ds(0, n_chunks)],
            send_sem=o_ss.at[0],
            recv_sem=o_rs.at[it],
            device_id={"ves": (v + 1) % n_ves},
            device_id_type=MESH,
        )

    barrier = pltpu.get_barrier_semaphore()

    def greet_ves(k, carry):
        pl.semaphore_signal(barrier, 1, device_id={"ves": ves_at(k)}, device_id_type=MESH)
        return carry

    def greet_tis(k, carry):
        pl.semaphore_signal(barrier, 1, device_id={"tis": tis_at(k)}, device_id_type=MESH)
        return carry

    lax.fori_loop(1, n_ves, greet_ves, 0)
    lax.fori_loop(1, 2 * n_z, greet_tis, 0)
    pl.semaphore_signal(barrier, 1, device_id={"tis": other_core}, device_id_type=MESH)

    solute = lax.broadcasted_iota(jnp.int32, (8, LANES), 0)
    lane = lax.broadcasted_iota(jnp.int32, (8, LANES), 1)

    def column(ref):
        out = jnp.zeros((8, LANES), f32)
        for s in range(8):
            out = jnp.where(solute == s, ref[s], out)
        return out

    half = column(half_ref)[:, :1]
    diff = column(diff_ref)[:, :1]
    base[...] = column(base_ref)

    def spread(out, rows, order):
        rows = jnp.concatenate(rows + [jnp.zeros((3, rows[0].shape[1]), f32)], axis=0)
        for a, piece in enumerate(pieces(rows)):
            for b in range(3):
                block = 3 * a + b if order else 3 * b + a
                out[8 * block : 8 * block + 8, :] = piece
        out[72:, :] = jnp.zeros((8, rows.shape[1]), f32)

    point = point_ref[...] - 0.5
    spread(
        feat, [point, jnp.sum(point * point, axis=0, keepdims=True), jnp.ones((1, pts), f32)], True
    )

    def turn(k):
        for i in range(chunk // LANES):
            cols = at(ves_at(k) * (chunk // LANES) + i, LANES)
            point_feat[cols, :] = feat[:, cols].T.astype(bf16)

    turn(n_ves - 1)

    segment = seg_ref[...] - 0.5
    square = jnp.sum(segment * segment, axis=0, keepdims=True) + radius_ref[...] * radius_ref[...]
    spread(feat_seg, [-2.0 * segment, jnp.ones((1, segs), f32), square], False)
    seg_feat[...] = feat_seg[...].astype(bf16)

    total = jnp.zeros((8, LANES), f32)
    for i in range(n_chunks):
        cols = slice(i * LANES, (i + 1) * LANES)
        total = total + sources_ref[:, cols]
    for k in range(n_ves):
        t_send[k, :, chunk:] = total

    def build(i, carry):
        k = n_ves - 1 - i
        rows = at(ves_at(k), chunk)
        turn((k + n_ves - 1) % n_ves)
        part = jnp.zeros((8, chunk), f32)
        for j in range(0, segs, quarter):
            cols = slice(j, j + quarter)
            block = lax.rsqrt(dot(point_feat[rows, :], seg_feat[:, cols])).astype(bf16)
            tile[rows, cols] = block
            part = part + dot_nt(sources_ref[:, cols].astype(bf16), block)
        t_send[k, :, :chunk] = part

        @pl.when(i == 0)
        def _():
            pl.semaphore_wait(barrier, n_ves - 1 + 2 * n_z)

        @pl.when(k > 0)
        def _():
            t_copy(0, k).start()

        return carry

    lax.fori_loop(0, n_ves, build, 0)
    table = table_ref[...]
    for i in range(pts // LANES):
        cell = jnp.broadcast_to(cell_ref[:, i * LANES : (i + 1) * LANES], (8, LANES))
        rates[:, i * LANES : (i + 1) * LANES] = jnp.take_along_axis(table, cell, axis=1)

    for i in range(n_chunks):
        cols = slice(i * LANES, (i + 1) * LANES)
        own, held = sources_ref[:, cols], contents_ref[:, cols]
        src[0, i // per_q, i % per_q] = own
        cont[i] = held
        joined[0, n_chunks + i] = held - own * flow_ref[:, cols]

    def sweep(it, carry):
        summed = t_send[0]
        for k in range(1, n_ves):
            t_copy(it, k).wait()
            summed = summed + t_recv[it, k - 1]
        level[it, v] = base[:, :1] + summed[:, :chunk] / (diff * total_segs)

        for k in range(n_ves - 1, 0, -1):
            l_copy(it, k, v).start()
        o_copy(it).start()
        sink_sum[...] = jnp.zeros_like(sink_sum)

        def sink_of(k):
            of = ves_from(k)

            @pl.when(k > 0)
            def _():
                l_copy(it, k, of).wait()

            now = level[it, of]
            value = rates[:, at(of, chunk)] * now / (jnp.abs(now) + half)
            sink[k] = value
            part = value[:, :LANES]
            for i in range(1, chunk // LANES):
                part = part + value[:, i * LANES : (i + 1) * LANES]
            sink_sum[...] += part
            return of

        wall[...] = jnp.zeros_like(wall)

        def early(k, carry):
            of = sink_of(k)
            wall[...] += dot(sink[k].astype(bf16), tile[at(of, chunk), :])
            return carry

        def late(k, carry):
            sink_of(k)
            return carry

        for k in range(n_early):
            early(k, 0)
        for k in range(n_early, n_ves):
            late(k, 0)

        sums = jnp.sum(sink_sum[...], axis=1, keepdims=True)
        sink_row = jnp.sum(jnp.where(solute == lane, sums, 0.0), axis=0, keepdims=True)
        for i in range(4):
            a_send[i, :, quarter:] = jnp.broadcast_to(sink_row, (8, LANES))

        def finish(i):
            cols = at(quarter_of(core + 1 + i // 2, y + 1 + i), quarter)
            part = wall[:, cols]
            for k in range(n_early, n_ves):
                of = ves_from(k)
                part = part + dot(sink[k].astype(bf16), tile[at(of, chunk), cols])
            a_send[i, :, :quarter] = part

        def give(i, carry):
            finish(i)
            a_copy(it, i).start()
            return carry

        for i in range(2):
            give(i, 0)

        def keep(i, carry):
            finish(2 + i)
            a_copy(it, i).wait()
            own = a_send[2 + i] + a_recv[it, i]
            for j in range(n_z):
                b_send[(y + 1 + i) % 2, j, :8, :] = own[:, j * LANES : (j + 1) * LANES]
                b_send[(y + 1 + i) % 2, j, 8:, :] = own[:1, quarter:]

            @pl.when(i == 0)
            def _():
                for k in far_first:
                    if k >= n_z:
                        b_copy(it, k).start()

            return carry

        for i in range(2):
            keep(i, 0)
        for k in far_first:
            if k < n_z:
                b_copy(it, k).start()

        o_copy(it).wait()

        def gather(c, carry):
            cols = at(c, LANES)
            parent = jnp.broadcast_to(parent_ref[:, cols], (8, LANES))
            root = parent == v * segs + c * LANES + lane
            offset = parent - (v * segs - segs) - c * LANES
            which, place = offset >> 7, offset & (LANES - 1)
            found = jnp.zeros((8, LANES), f32)
            for h in range(n_chunks + 1):
                found = jnp.where(which == h, jnp.take_along_axis(joined[it, c + h], place, axis=1), found)
            cont[c] = jnp.where(root, inflow_ref[:, cols], found)
            return carry

        lax.fori_loop(0, n_chunks, gather, 0)

        own = b_send[y, z]
        for k in range(1, 2 * n_z):
            b_copy(it, k).wait()
            own = own + b_recv[it, k - 1]
        q = quarter_of(core, y)
        cols = at(q * per_q + z, LANES)
        wall_field = own[:8] / (diff * total_pts)
        src[it + 1, q, z] = RELAX * src[it, q, z] + RELAX * cond_ref[:, cols] * (cont[q * per_q + z] - wall_field)
        for k in far_first:
            z_copy(it, k, q, z).start()
        source_total = jnp.sum(summed[:, chunk:], axis=1, keepdims=True)
        sink_total = jnp.sum(jnp.where(solute == lane, own[8:], 0.0), axis=1, keepdims=True)
        base[...] += BALANCE * (source_total / total_segs - sink_total / total_pts)

        def source_block(of):
            return jnp.concatenate([src[it + 1, of, i] for i in range(per_q)], axis=1).astype(bf16)

        def z_wait(q, step, of):
            k = step * n_z + (z + n_z - of) % n_z

            @pl.when(k > 0)
            def _():
                z_copy(it, k, q, of).wait()

        for step in range(n_pairs):
            pair = (z // 2 + near_first[step]) % n_pairs
            for e in range(2):
                z_wait(q, 0, pair * 2 + e)
            if step == n_pairs - 1:
                c_copy(it, 0, q).start()

            @pl.when(it < ITERS - 1)
            def _():
                two = jnp.concatenate([src[it + 1, q, pair * 2], src[it + 1, q, pair * 2 + 1]], axis=1).astype(bf16)
                part = dot_nt(two, tile[:, pl.ds(pl.multiple_of(q * quarter + pair * 2 * LANES, LANES), 2 * LANES)])
                if step == 0:
                    t_sum[...] = part
                else:
                    t_sum[...] += part

        q_next = quarter_of(core, y + 1)
        for of in range(n_z):
            z_wait(q_next, 1, of)
        c_copy(it, 1, q_next).start()

        @pl.when(it < ITERS - 1)
        def _():
            t_sum[...] += dot_nt(source_block(q_next), tile[:, at(q_next, quarter)])
            for i in range(2):
                c_copy(it, i, quarter_of(core + 1, y + i)).wait()

            total = jnp.zeros((8, LANES), f32)
            for i in range(n_chunks):
                cols = slice(i * LANES, (i + 1) * LANES)
                now = src[it + 1, i // per_q, i % per_q]
                joined[it + 1, n_chunks + i] = cont[i] - now * flow_ref[:, cols]
                total = total + now
            for k in range(n_ves):
                t_send[k, :, chunk:] = total
            there = (core + 1) % 2
            pair_block = jnp.concatenate([source_block(there * 2), source_block(there * 2 + 1)], axis=1)

            def last(i, carry):
                k = n_ves - 1 - i
                rows = at(ves_at(k), chunk)
                t_send[k, :, :chunk] = t_sum[:, rows] + dot_nt(pair_block, tile[rows, at(there, 2 * quarter)])

                @pl.when(k > 0)
                def _():
                    t_copy(it + 1, k).start()

                return carry

            for i in range(n_ves):
                last(i, 0)

        @pl.when(it == ITERS - 1)
        def _():
            for i in range(n_ves):
                level_out[:, i * chunk : (i + 1) * chunk] = level[it, i]
            for i in range(n_chunks):
                contents_out[:, i * LANES : (i + 1) * LANES] = cont[i]
            for i in range(2):
                c_copy(it, i, quarter_of(core + 1, y + i)).wait()
            for i in range(n_chunks):
                sources_out[:, i * LANES : (i + 1) * LANES] = src[it + 1, i // per_q, i % per_q]

        return carry

    lax.fori_loop(0, ITERS, sweep, 0)


def hand_over(a, b, c, a_out, b_out, c_out):
    a_out[...] = a[...]
    b_out[...] = b[...]
    c_out[...] = c[...]


def body(
    point_xyz,
    point_cell,
    seg_xyz,
    seg_radius,
    conductance,
    flow_inv,
    parent,
    inflow,
    rate_table,
    half_sat,
    diffusivity,
    base_level,
    sources,
    contents,
):
    n_ves = lax.axis_size("ves")
    n_z = lax.axis_size("tis") // 4
    pts, segs = point_xyz.shape[1], seg_xyz.shape[1]
    chunk, quarter, n_chunks = pts // n_ves, segs // 4, segs // LANES
    f32, bf16 = jnp.float32, jnp.bfloat16
    vmem = pl.BlockSpec(memory_space=pltpu.VMEM)
    smem = pl.BlockSpec(memory_space=pltpu.SMEM)
    sem = pltpu.SemaphoreType.DMA
    line = lambda x: x.reshape(1, -1)
    out = pl.pallas_call(
        functools.partial(kernel, n_ves, n_z, pts, segs),
        out_shape=(
            jax.ShapeDtypeStruct((8, pts), f32),
            jax.ShapeDtypeStruct((8, segs), f32),
            jax.ShapeDtypeStruct((8, segs), f32),
        ),
        in_specs=[vmem] * 9 + [smem] * 3 + [vmem] * 2,
        out_specs=(vmem, vmem, vmem),
        scratch_shapes=[
            pltpu.VMEM((pts, segs), bf16),
            pltpu.VMEM((pts, FEATURES), bf16),
            pltpu.VMEM((FEATURES, segs), bf16),
            pltpu.VMEM((FEATURES, pts), f32),
            pltpu.VMEM((FEATURES, segs), f32),
            pltpu.VMEM((8, pts), f32),
            pltpu.VMEM((8, LANES), f32),
            pltpu.VMEM((8, pts), f32),
            pltpu.VMEM((n_ves, 8, chunk + LANES), f32),
            pltpu.VMEM((ITERS, n_ves - 1, 8, chunk + LANES), f32),
            pltpu.VMEM((ITERS, n_ves, 8, chunk), f32),
            pltpu.VMEM((n_ves, 8, chunk), f32),
            pltpu.VMEM((8, LANES), f32),
            pltpu.VMEM((8, segs), f32),
            pltpu.VMEM((4, 8, quarter + LANES), f32),
            pltpu.VMEM((ITERS, 2, 8, quarter + LANES), f32),
            pltpu.VMEM((2, n_z, 9, LANES), f32),
            pltpu.VMEM((ITERS, 2 * n_z - 1, 9, LANES), f32),
            pltpu.VMEM((ITERS + 1, 4, n_z, 8, LANES), f32),
            pltpu.VMEM((n_chunks, 8, LANES), f32),
            pltpu.VMEM((ITERS, 2 * n_chunks, 8, LANES), f32),
            sem((n_ves - 1,)),
            sem((ITERS, n_ves - 1)),
            sem((n_ves - 1,)),
            sem((ITERS, n_ves - 1)),
            sem((2,)),
            sem((ITERS, 2)),
            sem((2 * n_z - 1,)),
            sem((ITERS, 2 * n_z - 1)),
            sem((2 * n_z - 1,)),
            sem((ITERS, 2 * n_z - 1)),
            sem((2,)),
            sem((ITERS, 2)),
            sem((1,)),
            sem((ITERS,)),
        ],
        compiler_params=pltpu.CompilerParams(
            collective_id=0, has_side_effects=True, vmem_limit_bytes=60 * 2**20
        ),
        name="exchange",
    )(
        point_xyz,
        line(point_cell),
        seg_xyz,
        line(seg_radius),
        line(conductance),
        line(flow_inv),
        line(parent),
        inflow,
        rate_table,
        half_sat,
        diffusivity,
        base_level,
        sources,
        contents,
    )
    return pl.pallas_call(
        hand_over,
        out_shape=tuple(jax.ShapeDtypeStruct(x.shape, f32) for x in out),
        in_specs=[vmem] * 3,
        out_specs=(vmem,) * 3,
        name="hand_over",
    )(*out)


def solution(mesh):
    return jax.shard_map(
        body,
        mesh=mesh,
        in_specs=(
            P(None, "tis"),
            P("tis"),
            P(None, "ves"),
            P("ves"),
            P("ves"),
            P("ves"),
            P("ves"),
            P(None, "ves"),
            P(),
            P(),
            P(),
            P(),
            P(None, "ves"),
            P(None, "ves"),
        ),
        out_specs=(P(None, "tis"), P(None, "ves"), P(None, "ves")),
        check_vma=False,
    )
```

```python
import functools

import jax
import jax.numpy as jnp
from jax import lax
from jax.experimental import pallas as pl
from jax.experimental.pallas import tpu as pltpu
from jax.sharding import PartitionSpec as P

ITERS = 3
RELAX = 0.5
BALANCE = 0.5
LANES = 128
FEATURES = 80
MESH = pl.DeviceIdType.MESH


def pieces(x):
    high = x.astype(jnp.bfloat16).astype(jnp.float32)
    rest = x - high
    middle = rest.astype(jnp.bfloat16).astype(jnp.float32)
    return high, middle, (rest - middle).astype(jnp.bfloat16).astype(jnp.float32)


def dot(a, b):
    return jnp.dot(a, b, preferred_element_type=jnp.float32)


def dot_nt(a, b):
    return lax.dot_general(a, b, (((1,), (1,)), ((), ())), preferred_element_type=jnp.float32)


def at(i, size):
    return pl.ds(pl.multiple_of(i * size, size), size)


def kernel(
    n_ves,
    n_z,
    pts,
    segs,
    point_ref,
    cell_ref,
    seg_ref,
    radius_ref,
    cond_ref,
    flow_ref,
    parent_ref,
    inflow_ref,
    table_ref,
    half_ref,
    diff_ref,
    base_ref,
    sources_ref,
    contents_ref,
    level_out,
    sources_out,
    contents_out,
    tile,
    point_feat,
    seg_feat,
    feat,
    feat_seg,
    rates,
    base,
    t_sum,
    t_send,
    t_recv,
    level,
    sink,
    sink_sum,
    wall,
    a_send,
    a_recv,
    b_send,
    b_recv,
    src,
    cont,
    joined,
    t_ss,
    t_rs,
    l_ss,
    l_rs,
    a_ss,
    a_rs,
    b_ss,
    b_rs,
    z_ss,
    z_rs,
    c_ss,
    c_rs,
    o_ss,
    o_rs,
):
    f32, bf16 = jnp.float32, jnp.bfloat16
    n_tis = 4 * n_z
    chunk = pts // n_ves
    quarter = segs // 4
    n_chunks = segs // LANES
    per_q = n_z
    total_pts = pts * n_tis
    total_segs = segs * n_ves
    t, v = lax.axis_index("tis"), lax.axis_index("ves")
    y, z, core = t // (2 * n_z), (t // 2) % n_z, t % 2

    def quarter_of(core, y):
        return core % 2 * 2 + y % 2

    def tis_at(k):
        return ((y + k // n_z) % 2) * (2 * n_z) + ((z + k % n_z) % n_z) * 2 + core

    other_core = y * (2 * n_z) + z * 2 + (core + 1) % 2

    n_x = n_ves // 2
    n_early = n_ves - max(1, n_ves * 3 // 8)
    n_pairs = n_z // 2
    v_y, v_x = v // n_x, v % n_x

    def ves_at(k):
        return ((v_y + k // n_x) % 2) * n_x + (v_x + k % n_x) % n_x

    def ves_from(k):
        return ((v_y + k // n_x) % 2) * n_x + (v_x + n_x - k % n_x) % n_x

    far_first = sorted(range(1, 2 * n_z), key=lambda k: -(k // n_z) - min(k % n_z, n_z - k % n_z))
    near_first = sorted(range(n_pairs), key=lambda k: min(k, n_pairs - k))

    def send_ves(k, a, b, s, r):
        return pltpu.make_async_remote_copy(
            src_ref=a, dst_ref=b, send_sem=s, recv_sem=r, device_id={"ves": ves_at(k)}, device_id_type=MESH
        )

    def send_tis(to, a, b, s, r):
        return pltpu.make_async_remote_copy(
            src_ref=a, dst_ref=b, send_sem=s, recv_sem=r, device_id={"tis": to}, device_id_type=MESH
        )

    def t_copy(it, k):
        return send_ves(k, t_send.at[k], t_recv.at[it, k - 1], t_ss.at[k - 1], t_rs.at[it, k - 1])

    def l_copy(it, k, of):
        return send_ves(k, level.at[it, of], level.at[it, of], l_ss.at[k - 1], l_rs.at[it, k - 1])

    def a_copy(it, i):
        return send_tis(other_core, a_send.at[i], a_recv.at[it, i], a_ss.at[i], a_rs.at[it, i])

    def b_copy(it, k):
        block = b_send.at[(y + k // n_z) % 2, (z + k % n_z) % n_z]
        return send_tis(tis_at(k), block, b_recv.at[it, k - 1], b_ss.at[k - 1], b_rs.at[it, k - 1])

    def z_copy(it, k, q, of):
        place = src.at[it + 1, q, of]
        return send_tis(tis_at(k), place, place, z_ss.at[k - 1], z_rs.at[it, k - 1])

    def c_copy(it, i, q):
        place = src.at[it + 1, q]
        return send_tis(other_core, place, place, c_ss.at[i], c_rs.at[it, i])

    def o_copy(it):
        return pltpu.make_async_remote_copy(
            src_ref=joined.at[it, pl.ds(n_chunks, n_chunks)],
            dst_ref=joined.at[it, pl.ds(0, n_chunks)],
            send_sem=o_ss.at[0],
            recv_sem=o_rs.at[it],
            device_id={"ves": (v + 1) % n_ves},
            device_id_type=MESH,
        )

    barrier = pltpu.get_barrier_semaphore()

    def greet_ves(k, carry):
        pl.semaphore_signal(barrier, 1, device_id={"ves": ves_at(k)}, device_id_type=MESH)
        return carry

    def greet_tis(k, carry):
        pl.semaphore_signal(barrier, 1, device_id={"tis": tis_at(k)}, device_id_type=MESH)
        return carry

    lax.fori_loop(1, n_ves, greet_ves, 0)
    lax.fori_loop(1, 2 * n_z, greet_tis, 0)
    pl.semaphore_signal(barrier, 1, device_id={"tis": other_core}, device_id_type=MESH)

    solute = lax.broadcasted_iota(jnp.int32, (8, LANES), 0)
    lane = lax.broadcasted_iota(jnp.int32, (8, LANES), 1)

    def column(ref):
        out = jnp.zeros((8, LANES), f32)
        for s in range(8):
            out = jnp.where(solute == s, ref[s], out)
        return out

    half = column(half_ref)[:, :1]
    diff = column(diff_ref)[:, :1]
    base[...] = column(base_ref)

    def spread(out, rows, order):
        rows = jnp.concatenate(rows + [jnp.zeros((3, rows[0].shape[1]), f32)], axis=0)
        for a, piece in enumerate(pieces(rows)):
            for b in range(3):
                block = 3 * a + b if order else 3 * b + a
                out[8 * block : 8 * block + 8, :] = piece
        out[72:, :] = jnp.zeros((8, rows.shape[1]), f32)

    point = point_ref[...] - 0.5
    spread(
        feat, [point, jnp.sum(point * point, axis=0, keepdims=True), jnp.ones((1, pts), f32)], True
    )

    def turn(k):
        for i in range(chunk // LANES):
            cols = at(ves_at(k) * (chunk // LANES) + i, LANES)
            point_feat[cols, :] = feat[:, cols].T.astype(bf16)

    turn(n_ves - 1)

    segment = seg_ref[...] - 0.5
    square = jnp.sum(segment * segment, axis=0, keepdims=True) + radius_ref[...] * radius_ref[...]
    spread(feat_seg, [-2.0 * segment, jnp.ones((1, segs), f32), square], False)
    seg_feat[...] = feat_seg[...].astype(bf16)

    total = jnp.zeros((8, LANES), f32)
    for i in range(n_chunks):
        cols = slice(i * LANES, (i + 1) * LANES)
        total = total + sources_ref[:, cols]
    for k in range(n_ves):
        t_send[k, :, chunk:] = total

    def build(i, carry):
        k = n_ves - 1 - i
        rows = at(ves_at(k), chunk)
        turn((k + n_ves - 1) % n_ves)
        part = jnp.zeros((8, chunk), f32)
        for j in range(0, segs, quarter):
            cols = slice(j, j + quarter)
            block = lax.rsqrt(dot(point_feat[rows, :], seg_feat[:, cols])).astype(bf16)
            tile[rows, cols] = block
            part = part + dot_nt(sources_ref[:, cols].astype(bf16), block)
        t_send[k, :, :chunk] = part

        @pl.when(i == 0)
        def _():
            pl.semaphore_wait(barrier, n_ves - 1 + 2 * n_z)

        @pl.when(k > 0)
        def _():
            t_copy(0, k).start()

        return carry

    lax.fori_loop(0, n_ves, build, 0)
    table = table_ref[...]
    for i in range(pts // LANES):
        cell = jnp.broadcast_to(cell_ref[:, i * LANES : (i + 1) * LANES], (8, LANES))
        rates[:, i * LANES : (i + 1) * LANES] = jnp.take_along_axis(table, cell, axis=1)

    for i in range(n_chunks):
        cols = slice(i * LANES, (i + 1) * LANES)
        own, held = sources_ref[:, cols], contents_ref[:, cols]
        src[0, i // per_q, i % per_q] = own
        cont[i] = held
        joined[0, n_chunks + i] = held - own * flow_ref[:, cols]

    def sweep(it, carry):
        summed = t_send[0]
        for k in range(1, n_ves):
            t_copy(it, k).wait()
            summed = summed + t_recv[it, k - 1]
        level[it, v] = base[:, :1] + summed[:, :chunk] / (diff * total_segs)

        for k in sorted(range(1, n_ves), key=lambda k: k // n_x * 2 + min(k % n_x, n_x - k % n_x)):
            l_copy(it, k, v).start()
        o_copy(it).start()
        sink_sum[...] = jnp.zeros_like(sink_sum)

        def sink_of(k):
            of = ves_from(k)

            @pl.when(k > 0)
            def _():
                l_copy(it, k, of).wait()

            now = level[it, of]
            value = rates[:, at(of, chunk)] * now / (jnp.abs(now) + half)
            sink[k] = value
            part = value[:, :LANES]
            for i in range(1, chunk // LANES):
                part = part + value[:, i * LANES : (i + 1) * LANES]
            sink_sum[...] += part
            return of

        wall[...] = jnp.zeros_like(wall)

        def early(k, carry):
            of = sink_of(k)
            wall[...] += dot(sink[k].astype(bf16), tile[at(of, chunk), :])
            return carry

        def late(k, carry):
            sink_of(k)
            return carry

        for k in range(n_early):
            early(k, 0)
        for k in range(n_early, n_ves):
            late(k, 0)

        sums = jnp.sum(sink_sum[...], axis=1, keepdims=True)
        sink_row = jnp.sum(jnp.where(solute == lane, sums, 0.0), axis=0, keepdims=True)
        for i in range(4):
            a_send[i, :, quarter:] = jnp.broadcast_to(sink_row, (8, LANES))

        def finish(i):
            cols = at(quarter_of(core + 1 + i // 2, y + 1 + i), quarter)
            part = wall[:, cols]
            for k in range(n_early, n_ves):
                of = ves_from(k)
                part = part + dot(sink[k].astype(bf16), tile[at(of, chunk), cols])
            a_send[i, :, :quarter] = part

        def give(i, carry):
            finish(i)
            a_copy(it, i).start()
            return carry

        for i in range(2):
            give(i, 0)

        def keep(i, carry):
            finish(2 + i)
            a_copy(it, i).wait()
            own = a_send[2 + i] + a_recv[it, i]
            for j in range(n_z):
                b_send[(y + 1 + i) % 2, j, :8, :] = own[:, j * LANES : (j + 1) * LANES]
                b_send[(y + 1 + i) % 2, j, 8:, :] = own[:1, quarter:]

            @pl.when(i == 0)
            def _():
                for k in far_first:
                    if k >= n_z:
                        b_copy(it, k).start()

            return carry

        for i in range(2):
            keep(i, 0)
        for k in far_first:
            if k < n_z:
                b_copy(it, k).start()

        o_copy(it).wait()

        def gather(c, carry):
            cols = at(c, LANES)
            parent = jnp.broadcast_to(parent_ref[:, cols], (8, LANES))
            root = parent == v * segs + c * LANES + lane
            offset = parent - (v * segs - segs) - c * LANES
            which, place = offset >> 7, offset & (LANES - 1)
            found = jnp.zeros((8, LANES), f32)
            for h in range(n_chunks + 1):
                found = jnp.where(which == h, jnp.take_along_axis(joined[it, c + h], place, axis=1), found)
            cont[c] = jnp.where(root, inflow_ref[:, cols], found)
            return carry

        lax.fori_loop(0, n_chunks, gather, 0)

        own = b_send[y, z]
        for k in range(1, 2 * n_z):
            b_copy(it, k).wait()
            own = own + b_recv[it, k - 1]
        q = quarter_of(core, y)
        cols = at(q * per_q + z, LANES)
        wall_field = own[:8] / (diff * total_pts)
        src[it + 1, q, z] = RELAX * src[it, q, z] + RELAX * cond_ref[:, cols] * (cont[q * per_q + z] - wall_field)
        for k in far_first:
            z_copy(it, k, q, z).start()
        source_total = jnp.sum(summed[:, chunk:], axis=1, keepdims=True)
        sink_total = jnp.sum(jnp.where(solute == lane, own[8:], 0.0), axis=1, keepdims=True)
        base[...] += BALANCE * (source_total / total_segs - sink_total / total_pts)

        def source_block(of):
            return jnp.concatenate([src[it + 1, of, i] for i in range(per_q)], axis=1).astype(bf16)

        def z_wait(q, step, of):
            k = step * n_z + (z + n_z - of) % n_z

            @pl.when(k > 0)
            def _():
                z_copy(it, k, q, of).wait()

        for step in range(n_pairs):
            pair = (z // 2 + near_first[step]) % n_pairs
            for e in range(2):
                z_wait(q, 0, pair * 2 + e)
            if step == n_pairs - 1:
                c_copy(it, 0, q).start()

            @pl.when(it < ITERS - 1)
            def _():
                two = jnp.concatenate([src[it + 1, q, pair * 2], src[it + 1, q, pair * 2 + 1]], axis=1).astype(bf16)
                part = dot_nt(two, tile[:, pl.ds(pl.multiple_of(q * quarter + pair * 2 * LANES, LANES), 2 * LANES)])
                if step == 0:
                    t_sum[...] = part
                else:
                    t_sum[...] += part

        q_next = quarter_of(core, y + 1)
        for of in range(n_z):
            z_wait(q_next, 1, of)
        c_copy(it, 1, q_next).start()

        @pl.when(it < ITERS - 1)
        def _():
            t_sum[...] += dot_nt(source_block(q_next), tile[:, at(q_next, quarter)])
            for i in range(2):
                c_copy(it, i, quarter_of(core + 1, y + i)).wait()

            total = jnp.zeros((8, LANES), f32)
            for i in range(n_chunks):
                cols = slice(i * LANES, (i + 1) * LANES)
                now = src[it + 1, i // per_q, i % per_q]
                joined[it + 1, n_chunks + i] = cont[i] - now * flow_ref[:, cols]
                total = total + now
            for k in range(n_ves):
                t_send[k, :, chunk:] = total
            there = (core + 1) % 2
            pair_block = jnp.concatenate([source_block(there * 2), source_block(there * 2 + 1)], axis=1)

            def last(i, carry):
                k = n_ves - 1 - i
                rows = at(ves_at(k), chunk)
                t_send[k, :, :chunk] = t_sum[:, rows] + dot_nt(pair_block, tile[rows, at(there, 2 * quarter)])

                @pl.when(k > 0)
                def _():
                    t_copy(it + 1, k).start()

                return carry

            for i in range(n_ves):
                last(i, 0)

        @pl.when(it == ITERS - 1)
        def _():
            for i in range(n_ves):
                level_out[:, i * chunk : (i + 1) * chunk] = level[it, i]
            for i in range(n_chunks):
                contents_out[:, i * LANES : (i + 1) * LANES] = cont[i]
            for i in range(2):
                c_copy(it, i, quarter_of(core + 1, y + i)).wait()
            for i in range(n_chunks):
                sources_out[:, i * LANES : (i + 1) * LANES] = src[it + 1, i // per_q, i % per_q]

        return carry

    lax.fori_loop(0, ITERS, sweep, 0)


def hand_over(a, b, c, a_out, b_out, c_out):
    a_out[...] = a[...]
    b_out[...] = b[...]
    c_out[...] = c[...]


def body(
    point_xyz,
    point_cell,
    seg_xyz,
    seg_radius,
    conductance,
    flow_inv,
    parent,
    inflow,
    rate_table,
    half_sat,
    diffusivity,
    base_level,
    sources,
    contents,
):
    n_ves = lax.axis_size("ves")
    n_z = lax.axis_size("tis") // 4
    pts, segs = point_xyz.shape[1], seg_xyz.shape[1]
    chunk, quarter, n_chunks = pts // n_ves, segs // 4, segs // LANES
    f32, bf16 = jnp.float32, jnp.bfloat16
    vmem = pl.BlockSpec(memory_space=pltpu.VMEM)
    smem = pl.BlockSpec(memory_space=pltpu.SMEM)
    sem = pltpu.SemaphoreType.DMA
    line = lambda x: x.reshape(1, -1)
    out = pl.pallas_call(
        functools.partial(kernel, n_ves, n_z, pts, segs),
        out_shape=(
            jax.ShapeDtypeStruct((8, pts), f32),
            jax.ShapeDtypeStruct((8, segs), f32),
            jax.ShapeDtypeStruct((8, segs), f32),
        ),
        in_specs=[vmem] * 9 + [smem] * 3 + [vmem] * 2,
        out_specs=(vmem, vmem, vmem),
        scratch_shapes=[
            pltpu.VMEM((pts, segs), bf16),
            pltpu.VMEM((pts, FEATURES), bf16),
            pltpu.VMEM((FEATURES, segs), bf16),
            pltpu.VMEM((FEATURES, pts), f32),
            pltpu.VMEM((FEATURES, segs), f32),
            pltpu.VMEM((8, pts), f32),
            pltpu.VMEM((8, LANES), f32),
            pltpu.VMEM((8, pts), f32),
            pltpu.VMEM((n_ves, 8, chunk + LANES), f32),
            pltpu.VMEM((ITERS, n_ves - 1, 8, chunk + LANES), f32),
            pltpu.VMEM((ITERS, n_ves, 8, chunk), f32),
            pltpu.VMEM((n_ves, 8, chunk), f32),
            pltpu.VMEM((8, LANES), f32),
            pltpu.VMEM((8, segs), f32),
            pltpu.VMEM((4, 8, quarter + LANES), f32),
            pltpu.VMEM((ITERS, 2, 8, quarter + LANES), f32),
            pltpu.VMEM((2, n_z, 9, LANES), f32),
            pltpu.VMEM((ITERS, 2 * n_z - 1, 9, LANES), f32),
            pltpu.VMEM((ITERS + 1, 4, n_z, 8, LANES), f32),
            pltpu.VMEM((n_chunks, 8, LANES), f32),
            pltpu.VMEM((ITERS, 2 * n_chunks, 8, LANES), f32),
            sem((n_ves - 1,)),
            sem((ITERS, n_ves - 1)),
            sem((n_ves - 1,)),
            sem((ITERS, n_ves - 1)),
            sem((2,)),
            sem((ITERS, 2)),
            sem((2 * n_z - 1,)),
            sem((ITERS, 2 * n_z - 1)),
            sem((2 * n_z - 1,)),
            sem((ITERS, 2 * n_z - 1)),
            sem((2,)),
            sem((ITERS, 2)),
            sem((1,)),
            sem((ITERS,)),
        ],
        compiler_params=pltpu.CompilerParams(
            collective_id=0, has_side_effects=True, vmem_limit_bytes=60 * 2**20
        ),
        name="exchange",
    )(
        point_xyz,
        line(point_cell),
        seg_xyz,
        line(seg_radius),
        line(conductance),
        line(flow_inv),
        line(parent),
        inflow,
        rate_table,
        half_sat,
        diffusivity,
        base_level,
        sources,
        contents,
    )
    return pl.pallas_call(
        hand_over,
        out_shape=tuple(jax.ShapeDtypeStruct(x.shape, f32) for x in out),
        in_specs=[vmem] * 3,
        out_specs=(vmem,) * 3,
        name="hand_over",
    )(*out)


def solution(mesh):
    return jax.shard_map(
        body,
        mesh=mesh,
        in_specs=(
            P(None, "tis"),
            P("tis"),
            P(None, "ves"),
            P("ves"),
            P("ves"),
            P("ves"),
            P("ves"),
            P(None, "ves"),
            P(),
            P(),
            P(),
            P(),
            P(None, "ves"),
            P(None, "ves"),
        ),
        out_specs=(P(None, "tis"), P(None, "ves"), P(None, "ves")),
        check_vma=False,
    )
```
